256 devices in a mesh: pb: 16 (over y, x), kv: 16 (over z, core).
Axes of the slice: x: 4, y: 4, z: 8, core: 2. Of those that a mesh axis runs over, the one named last changes fastest.
Arguments:
- query: bfloat16 [4096, 128, 192], P('pb', 'kv'), may hold values from -12 to 12
- w_uk: bfloat16 [128, 128, 512], P('kv'), may hold values from -0.5 to 0.5
- w_uv: bfloat16 [128, 512, 128], P('kv'), may hold values from -1 to 1
- kv_cache: bfloat16 [32768, 576], P('kv'), may hold values from -6 to 6
- stretch_latent: bfloat16 [4096, 576], P('pb'), may hold values from -6 to 6
- selection: int32 [64, 30], P('pb'), may hold values from 0 to 511, as said below
Outputs:
- attended: bfloat16 [4096, 16384], P('pb', 'kv')
The draws below stay inside these ranges and needn't reach their ends.
Inputs may be any that keep to these rules, and one draw needn't show every extreme that they name: `selection`: each row lists 30 distinct cached blocks in increasing order; of one row at most 3 lie among the blocks j * 32 to (j + 1) * 32 - 1 of any j, and in every row some j holds exactly 3.
All inputs are finite; a program needn't handle non-finite values.
Results may differ from the reference program's by a relative error of at most 0.009.
Values may be sent and summed in bfloat16 or wider, within the bound.
A program may use at most 128 MiB of HBM per device.

```python
import math
import jax
import jax.numpy as jnp
from jax import lax

H = 128
NOPE = 128
ROPE = 64
LATENT = 512
VDIM = 128
BLOCK = 64
WIN = 2
KB_DEV = 32
TOKENS = 4096
NQB = 64
NKB = 512
PRIOR = 32768
SELB = 30
CAP = 3
N_KV = 16


def draw_query(key, part):
    key = jax.random.fold_in(key, 11)
    values = jax.random.truncated_normal(key, -6.0, 6.0, (TOKENS, H, NOPE + ROPE), jnp.float32)
    return values.astype(jnp.bfloat16)


def draw_stretch_latent(key, part):
    key = jax.random.fold_in(key, 23)
    values = jax.random.truncated_normal(key, -6.0, 6.0, (TOKENS, LATENT + ROPE), jnp.float32)
    return values.astype(jnp.bfloat16)


def draw_selection(key, part):
    key = jax.random.fold_in(key, 37)
    first, second = jax.random.split(key)
    order = jax.vmap(lambda k: jax.random.permutation(k, NKB))(jax.random.split(first, NQB)).astype(jnp.int32)
    hot = jax.random.randint(second, (NQB,), 0, N_KV)
    holder = jnp.arange(NKB, dtype=jnp.int32) // KB_DEV
    boosted = order + jnp.where(holder[None, :] == hot[:, None], NKB, 0).astype(jnp.int32)
    grouped = boosted.reshape(NQB, N_KV, KB_DEV)
    rank = jnp.sum((grouped[:, :, None, :] > grouped[:, :, :, None]).astype(jnp.int32), axis=3)
    eligible = (rank < CAP).reshape(NQB, NKB)
    score = jnp.where(eligible, boosted, -1)
    best, index = lax.top_k(score, SELB)
    return jnp.sort(index.astype(jnp.int32), axis=1)


def shard_levels(own_key, dims, pieces, low, top_value):
    level = 1.0
    for axis_at, blocks in pieces:
        steps = jax.random.uniform(jax.random.fold_in(jax.random.fold_in(own_key, 6), axis_at), (blocks,), jnp.float32, low / len(pieces), top_value / len(pieces))
        level = level * jnp.repeat(jnp.exp(steps), dims[axis_at] // blocks).reshape((-1,) + (1,) * (len(dims) - 1 - axis_at))
    return level


def bell_draw(rng, extent, spread, bound, pieces=(), kind=jnp.bfloat16):
    entries = spread * jax.random.normal(rng, extent, jnp.float32)
    if pieces:
        entries = entries * shard_levels(rng, extent, pieces, -0.22, 0.18)
    return jnp.clip(entries, -bound, bound).astype(kind)


def setup_inputs(seed: int = 0) -> dict:
    keys = jax.random.split(jax.random.key(seed), 7)
    query = draw_query(jax.random.fold_in(keys[6], 71), 0)
    w_uk = bell_draw(keys[1], (H, NOPE, LATENT), NOPE ** -0.5, 0.5, ((0, 16),))
    w_uv = bell_draw(keys[2], (H, LATENT, VDIM), (LATENT // 16) ** -0.5, 1.0, ((0, 16),))
    kv_cache = bell_draw(keys[3], (PRIOR, LATENT + ROPE), 1.0, 6.0, ((0, 16),))
    stretch_latent = draw_stretch_latent(jax.random.fold_in(keys[6], 71), 0)
    selection = draw_selection(jax.random.fold_in(keys[6], 71), 0)
    return {"query": query, "w_uk": w_uk, "w_uv": w_uv, "kv_cache": kv_cache, "stretch_latent": stretch_latent, "selection": selection}


def absorb(query, w_uk):
    plain = query[:, :, :NOPE].astype(jnp.float32)
    absorbed = jnp.einsum('thn,hnl->thl', plain, w_uk.astype(jnp.float32)).astype(jnp.bfloat16)
    absorbed = lax.optimization_barrier(absorbed)
    return jnp.concatenate([absorbed, query[:, :, NOPE:]], axis=2)

def reference(query, w_uk, w_uv, kv_cache, stretch_latent, selection):
    width = LATENT + ROPE
    full = absorb(query, w_uk)
    grouped = full.reshape(NQB, BLOCK, H, width)
    cache_blocks = kv_cache.reshape(NKB, BLOCK, width)
    padded = jnp.concatenate([jnp.zeros(((WIN - 1) * BLOCK, width), jnp.bfloat16), stretch_latent], axis=0)
    softmax_scale = 1.0 / math.sqrt(NOPE + ROPE)

    def single_block(g):
        query_rows = grouped[g].astype(jnp.float32)
        chosen = cache_blocks[selection[g]].reshape(SELB * BLOCK, width)
        recent = lax.dynamic_slice_in_dim(padded, g * BLOCK, WIN * BLOCK, 0)
        key_rows = jnp.concatenate([chosen, recent], axis=0)
        key_index = (g - WIN + 1) * BLOCK + jnp.arange(WIN * BLOCK, dtype=jnp.int32)
        query_index = g * BLOCK + jnp.arange(BLOCK, dtype=jnp.int32)
        near = (key_index[None, :] >= 0) & (key_index[None, :] <= query_index[:, None])
        valid = jnp.concatenate([jnp.ones((BLOCK, SELB * BLOCK), bool), near], axis=1)
        logit_scores = jnp.einsum('thd,kd->thk', query_rows, key_rows.astype(jnp.float32)) * softmax_scale
        logit_scores = jnp.where(valid[:, None, :], logit_scores, -jnp.inf)
        largest = lax.optimization_barrier(jnp.max(logit_scores, axis=2, keepdims=True))
        weights = jnp.exp(logit_scores - largest)
        total = lax.optimization_barrier(jnp.sum(weights, axis=2, keepdims=True))
        rounded = lax.optimization_barrier(weights.astype(jnp.bfloat16)).astype(jnp.float32)
        latent_out = jnp.einsum('thk,kl->thl', rounded, key_rows[:, :LATENT].astype(jnp.float32)) / total
        return latent_out.astype(jnp.bfloat16)
    latent_out = lax.map(single_block, jnp.arange(NQB, dtype=jnp.int32)).reshape(TOKENS, H, LATENT)
    latent_out = lax.optimization_barrier(latent_out)
    attended = jnp.einsum('thl,hlv->thv', latent_out.astype(jnp.float32), w_uv.astype(jnp.float32))
    return attended.astype(jnp.bfloat16).reshape(TOKENS, H * VDIM)
```

```python
import functools
import math

import jax
import jax.numpy as jnp
from jax import lax
from jax.experimental import pallas as pl
from jax.experimental.pallas import tpu as pltpu
from jax.sharding import PartitionSpec as P

NOPE = 128
ROPE = 64
LATENT = 512
WIDTH = LATENT + ROPE
VDIM = 128
BLOCK = 64
LANES = 128
CAP = 3
NEG = -1e30
MESH = pl.DeviceIdType.MESH
F32 = jnp.float32
BF16 = jnp.bfloat16


def transposed_dot(a, b):
    return lax.dot_general(a, b, (((0,), (0,)), ((), ())), preferred_element_type=F32)


def swap_halves(x):
    return jnp.concatenate([x[:, BLOCK:], x[:, :BLOCK]], axis=1)


def kernel(
    pb_total, kv_total, scale,
    sel_ref, query_hbm, uk_hbm, uv_hbm, kv_hbm, near_hbm,
    out_ref,
    kv_v, query_v, uk_v, uv_v, near_v, before_v, full_v, ring_v, twin_v, acc_v, top_v, total_v, latent_v, count_ref,
    load_sem, kv_sem, near_send, near_recv, ring_send, ring_recv, twin_send, twin_recv,
):
    heads = query_v.shape[0]
    tok = query_v.shape[2]
    blocks = tok // BLOCK
    pairs = blocks // 2
    chips = kv_total // 2
    kb_dev = 2 * kv_v.shape[0]
    pb = lax.axis_index("pb")
    kv = lax.axis_index("kv")
    chip = kv // 2
    core = kv % 2
    ahead = (chip + 1 - 2 * core + chips) % chips
    behind = (chip - 1 + 2 * core + chips) % chips
    to_next = (pb, 2 * ahead + core)
    to_prev = (pb, 2 * behind + core)
    to_twin = (pb, 2 * chip + 1 - core)
    to_right = ((pb + 1) % pb_total, kv)
    to_left = ((pb + pb_total - 1) % pb_total, kv)

    def load_kv(i):
        return pltpu.make_async_copy(
            kv_hbm.at[:, pl.ds(i * LANES, LANES)], kv_v.at[i], kv_sem.at[i]
        )

    load_near = pltpu.make_async_copy(near_hbm, near_v, load_sem.at[0])
    load_query = pltpu.make_async_copy(query_hbm, query_v, load_sem.at[1])
    load_uk = pltpu.make_async_copy(uk_hbm, uk_v, load_sem.at[2])
    load_uv = pltpu.make_async_copy(uv_hbm, uv_v, load_sem.at[3])
    for i in range(kv_v.shape[0]):
        load_kv(i).start()
    load_near.start()
    load_query.start()
    load_uk.start()
    load_uv.start()

    barrier = pltpu.get_barrier_semaphore()
    partners = (to_next, to_prev, to_twin, to_right, to_left)
    for partner in partners:
        pl.semaphore_signal(barrier, inc=1, device_id=partner, device_id_type=MESH)

    low = lax.broadcasted_iota(jnp.int32, (WIDTH, LANES), 1) < BLOCK

    def ring_copy(step, pair):
        slot = step * pairs + pair
        return pltpu.make_async_remote_copy(
            src_ref=ring_v.at[slot], dst_ref=ring_v.at[slot + pairs],
            send_sem=ring_send.at[slot], recv_sem=ring_recv.at[slot + pairs],
            device_id=to_next, device_id_type=MESH,
        )

    def twin_copy(slot):
        return pltpu.make_async_remote_copy(
            src_ref=ring_v.at[slot], dst_ref=twin_v.at[slot],
            send_sem=twin_send.at[slot], recv_sem=twin_recv.at[slot],
            device_id=to_twin, device_id_type=MESH,
        )

    selected = sel_ref.shape[1]

    def selected_below(row, bound):
        found = jnp.int32(0)
        for i in range(selected):
            found += jnp.where(sel_ref[row, i] < bound, 1, 0)
        return found

    first_own = [selected_below(row, kv * kb_dev) for row in range(blocks)]

    def local_block(pair, flip, slot):
        row = 2 * pair + flip
        start = jnp.where(flip == 0, first_own[2 * pair], first_own[2 * pair + 1])
        place = jnp.minimum(start + slot, selected - 1)
        return jnp.clip(sel_ref[row, place] - kv * kb_dev, 0, kb_dev - 1)

    def fetch(block):
        return kv_v[block >> 1], block & 1

    for i in range(kv_v.shape[0]):
        load_kv(i).wait()
    for pair in range(pairs):
        for slot in range(CAP):
            tile, odd = fetch(local_block(pair, core, slot))
            left = jnp.where(odd == 1, swap_halves(tile), tile)
            tile, odd = fetch(local_block(pair, 1 - core, slot))
            right = jnp.where(odd == 0, swap_halves(tile), tile)
            ring_v[pair, slot] = jnp.where(low, left, right)
        if pair == 0:
            pl.semaphore_wait(barrier, len(partners))
        ring_copy(0, pair).start()
        twin_copy(pair).start()

    load_near.wait()
    near_copy = pltpu.make_async_remote_copy(
        src_ref=near_v.at[:, pl.ds(tok - LANES, LANES)], dst_ref=before_v,
        send_sem=near_send, recv_sem=near_recv,
        device_id=to_right, device_id_type=MESH,
    )
    near_copy.start()

    load_query.wait()
    load_uk.wait()

    def prepare(j, _):
        full = []
        for i in range(2):
            h = 2 * j + i
            absorbed = transposed_dot(uk_v[h], query_v[h, :NOPE, :]).astype(BF16)
            full.append(jnp.concatenate([absorbed, query_v[h, NOPE:, :]], axis=0))
        column = pl.ds(pl.multiple_of(j * LANES, LANES), LANES)
        for pair in range(pairs):
            a = full[0][:, pair * LANES : (pair + 1) * LANES]
            b = full[1][:, pair * LANES : (pair + 1) * LANES]
            full_v[2 * pair, :, column] = jnp.where(low, a, swap_halves(b))
            full_v[2 * pair + 1, :, column] = jnp.where(low, swap_halves(a), b)
        share = kv_total // (heads // 2)
        for row in range(blocks):
            below = selected_below(row, j * share * kb_dev)
            for i in range(share):
                holder = j * share + i
                upto = selected_below(row, (holder + 1) * kb_dev)
                count_ref[row, holder] = upto - below
                below = upto
        return 0

    lax.fori_loop(0, heads // 2, prepare, 0)

    rows = heads * BLOCK
    near_copy.wait_recv()
    token = lax.broadcasted_iota(jnp.int32, (BLOCK, rows), 1) % BLOCK
    entry = lax.broadcasted_iota(jnp.int32, (BLOCK, rows), 0)
    causal = entry <= token
    for row in range(blocks):
        tile = near_v[:, (row // 2) * LANES : (row // 2 + 1) * LANES]
        if row % 2 == 0:
            other = before_v[...] if row == 0 else near_v[:, (row // 2 - 1) * LANES : (row // 2) * LANES]
            tile = jnp.where(low, tile, other)
        scores = transposed_dot(tile, full_v[row]) * scale
        first, second = scores[:BLOCK], scores[BLOCK:]
        if row % 2 == 0:
            first = jnp.where(causal, first, NEG)
            if row == 0:
                second = jnp.where(pb > 0, second, NEG)
        else:
            second = jnp.where(causal, second, NEG)
        scores = jnp.concatenate([first, second], axis=0)
        top = jnp.max(scores, axis=0, keepdims=True)
        weights = jnp.exp2(scores - top)
        top_v[row] = top
        total_v[row] = jnp.sum(weights, axis=0, keepdims=True)
        acc_v[row] = jnp.dot(tile[:LATENT], weights.astype(BF16), preferred_element_type=F32)

    def fold(slot):
        step = slot // pairs
        pair = slot % pairs
        plus = (chip - step + chips) % chips
        minus = (chip + step) % chips
        mine = jnp.where(core == 0, 2 * plus, 2 * minus + 1)
        other = jnp.where(core == 0, 2 * minus + 1, 2 * plus)
        for half in range(2):
            row = 2 * pair + half
            mine_low = core == half
            tiles = []
            for s in range(CAP):
                own, twin = ring_v[slot, s], twin_v[slot, s]
                tiles.append(jnp.where(low == mine_low, own, twin))
            keys = jnp.concatenate(tiles, axis=1)
            low_count = jnp.where(mine_low, count_ref[row, mine], count_ref[row, other])
            high_count = jnp.where(mine_low, count_ref[row, other], count_ref[row, mine])
            scores = transposed_dot(keys, full_v[row]) * scale
            parts = []
            for s in range(CAP):
                at = 2 * s * BLOCK
                parts.append(jnp.where(low_count > s, scores[at : at + BLOCK], NEG))
                parts.append(jnp.where(high_count > s, scores[at + BLOCK : at + 2 * BLOCK], NEG))
            scores = jnp.concatenate(parts, axis=0)
            old = top_v[row]
            top = jnp.maximum(old, jnp.max(scores, axis=0, keepdims=True))
            weights = jnp.exp2(scores - top)
            factor = jnp.exp2(old - top)
            top_v[row] = top
            total_v[row] = total_v[row] * factor + jnp.sum(weights, axis=0, keepdims=True)
            acc_v[row] = acc_v[row] * factor + jnp.dot(
                keys[:LATENT], weights.astype(BF16), preferred_element_type=F32
            )

    def stage(slot, _):
        step = slot // pairs
        pair = slot % pairs
        ring_copy(step - 1, pair).wait_recv()

        @pl.when(step < chips - 1)
        def _():
            ring_copy(step, pair).start()

        twin_copy(slot).start()
        twin_copy(slot - pairs).wait_recv()
        fold(slot - pairs)
        return 0

    slots = chips * pairs
    lax.fori_loop(pairs, slots, stage, 0)
    for slot in range(slots - pairs, slots):
        twin_copy(slot).wait_recv()
        fold(slot)

    load_uv.wait()
    for row in range(blocks):
        latent = (acc_v[row] * (1.0 / total_v[row])).astype(BF16)
        for j in range(heads // 2):
            tile = latent[:, j * LANES : (j + 1) * LANES].T
            for i in range(2):
                latent_v[2 * j + i, row * BLOCK : (row + 1) * BLOCK, :] = tile[i * BLOCK : (i + 1) * BLOCK]
    for h in range(heads):
        out_ref[:, h * VDIM : (h + 1) * VDIM] = jnp.dot(
            latent_v[h], uv_v[h], preferred_element_type=F32
        ).astype(BF16)

    near_copy.wait_send()

    def drain(slot, _):
        @pl.when(slot < slots - pairs)
        def _():
            ring_copy(slot // pairs, slot % pairs).wait_send()

        twin_copy(slot).wait_send()
        return 0

    lax.fori_loop(0, slots, drain, 0)


def per_device(query, w_uk, w_uv, kv_cache, stretch_latent, selection):
    pb_total = lax.axis_size("pb")
    kv_total = lax.axis_size("kv")
    tok, heads, qwidth = query.shape
    blocks = tok // BLOCK
    pairs = blocks // 2
    chips = kv_total // 2
    scale = math.log2(math.e) / math.sqrt(qwidth)
    slots = chips * pairs
    smem = pl.BlockSpec(memory_space=pltpu.SMEM)
    anywhere = pl.BlockSpec(memory_space=pl.ANY)
    dma = pltpu.SemaphoreType.DMA
    return pl.pallas_call(
        functools.partial(kernel, pb_total, kv_total, scale),
        out_shape=jax.ShapeDtypeStruct((tok, heads * VDIM), BF16),
        in_specs=[smem] + [anywhere] * 5,
        out_specs=pl.BlockSpec(memory_space=pltpu.VMEM),
        scratch_shapes=[
            pltpu.VMEM((kv_cache.shape[0] // LANES, WIDTH, LANES), BF16),
            pltpu.VMEM((heads, qwidth, tok), BF16),
            pltpu.VMEM(w_uk.shape, BF16),
            pltpu.VMEM(w_uv.shape, BF16),
            pltpu.VMEM((WIDTH, tok), BF16),
            pltpu.VMEM((WIDTH, LANES), BF16),
            pltpu.VMEM((blocks, WIDTH, heads * BLOCK), BF16),
            pltpu.VMEM((slots, CAP, WIDTH, LANES), BF16),
            pltpu.VMEM((slots, CAP, WIDTH, LANES), BF16),
            pltpu.VMEM((blocks, LATENT, heads * BLOCK), F32),
            pltpu.VMEM((blocks, 1, heads * BLOCK), F32),
            pltpu.VMEM((blocks, 1, heads * BLOCK), F32),
            pltpu.VMEM((heads, tok, LATENT), BF16),
            pltpu.SMEM((blocks, kv_total), jnp.int32),
            dma((4,)),
            dma((kv_cache.shape[0] // LANES,)),
            dma,
            dma,
            dma((slots,)),
            dma((slots,)),
            dma((slots,)),
            dma((slots,)),
        ],
        compiler_params=pltpu.CompilerParams(
            collective_id=0, has_side_effects=True, vmem_limit_bytes=56 * 1024 * 1024
        ),
        cost_estimate=pl.CostEstimate(
            flops=2 * blocks * heads * BLOCK * 3200 * (WIDTH + LATENT),
            bytes_accessed=8 * 1024 * 1024,
            transcendentals=blocks * heads * BLOCK * 3200,
        ),
    )(
        selection,
        jnp.transpose(query, (1, 2, 0)),
        w_uk,
        w_uv,
        kv_cache.T,
        stretch_latent.T,
    )


def solution(mesh):
    placed = (
        P("pb", "kv", None),
        P("kv", None, None),
        P("kv", None, None),
        P("kv", None),
        P("pb", None),
        P("pb", None),
    )
    return jax.shard_map(
        per_device, mesh=mesh, in_specs=placed, out_specs=P("pb", "kv"), check_vma=False
    )
```

```python
import functools
import math

import jax
import jax.numpy as jnp
from jax import lax
from jax.experimental import pallas as pl
from jax.experimental.pallas import tpu as pltpu
from jax.sharding import PartitionSpec as P

NOPE = 128
ROPE = 64
LATENT = 512
WIDTH = LATENT + ROPE
VDIM = 128
BLOCK = 64
LANES = 128
CAP = 3
SIDE = 4
NEG = -1e30
MESH = pl.DeviceIdType.MESH
F32 = jnp.float32
BF16 = jnp.bfloat16


def transposed_dot(a, b):
    return lax.dot_general(a, b, (((0,), (0,)), ((), ())), preferred_element_type=F32)


def swap_halves(x):
    return jnp.concatenate([x[:, BLOCK:], x[:, :BLOCK]], axis=1)


def kernel(
    pb_total, kv_total, scale,
    sel_ref, query_hbm, uk_hbm, uv_hbm, kv_hbm, near_hbm,
    out_ref,
    kv_v, far0_v, far1_v, far2_v, query_v, uk_v, uv_v, near_v, before_v, full_v, slots_v, twin_v,
    acc_v, top_v, total_v, latent_v, start_ref, count_ref,
    load_sem, kv_sem, near_send, near_recv, z_send, z_recv, twin_send, twin_recv,
    chain_send, chain_recv, line_send, line_recv,
):
    far_v = (far0_v, far1_v, far2_v)
    heads = query_v.shape[0]
    tok = query_v.shape[2]
    blocks = tok // BLOCK
    pairs = blocks // 2
    chips = kv_total // 2
    kb_dev = 2 * kv_v.shape[0]
    selected = sel_ref.shape[1]
    pb = lax.axis_index("pb")
    kv = lax.axis_index("kv")
    chip = kv // 2
    core = kv % 2
    turn = 1 - 2 * core
    half_width = WIDTH // 2

    def along_z(steps):
        return (pb, 2 * ((chip + steps + 2 * chips) % chips) + core)

    x, y = pb % SIDE, pb // SIDE
    a = (1 - core) * x + core * y
    s = (1 - core) * y + core * x
    place = s * SIDE + a

    def plane(da, ds):
        na, ns = (a + da + SIDE) % SIDE, (s + ds + SIDE) % SIDE
        return ((1 - core) * (ns * SIDE + na) + core * (na * SIDE + ns), kv)

    to_twin = (pb, 2 * chip + 1 - core)
    up, down = along_z(1), along_z(-1)
    right1, left1, right2, left2 = plane(1, 0), plane(-1, 0), plane(0, 1), plane(0, -1)
    to_right = ((pb + 1) % pb_total, kv)
    to_left = ((pb + pb_total - 1) % pb_total, kv)

    def remote(src, dst, send_sem, recv_sem, device):
        return pltpu.make_async_remote_copy(
            src_ref=src, dst_ref=dst, send_sem=send_sem, recv_sem=recv_sem,
            device_id=device, device_id_type=MESH,
        )

    def z_copy(n, side):
        pair, c = n // CAP % 2, n % CAP
        first = 2 + 4 * pair + side
        src, dst = (pair, first) if n < 2 * CAP else (first, 10 + 4 * pair + side)
        at = 2 * n + side
        return remote(
            slots_v.at[src, c], slots_v.at[dst, c], z_send.at[at], z_recv.at[at], (up, down)[side]
        )

    def z_go(*tiles):
        for n in tiles:
            for side in range(2):
                z_copy(n, side).start()

    def twin_copy(slot):
        return remote(slots_v.at[slot], twin_v.at[slot], twin_send.at[slot], twin_recv.at[slot], to_twin)

    def chain_copy(f):
        tile = kv_hbm.at[:, pl.ds(place * LANES, LANES)] if f == 0 else far_v[f - 1].at[place]
        return remote(
            tile, far_v[f].at[place], chain_send.at[f], chain_recv.at[f],
            along_z(3 * turn if f == 0 else turn),
        )

    def line_copy(f, n, side):
        buf = far_v[f]
        back = 2 * side - 1
        rows = pl.ds(side * half_width, half_width)
        shift = (0, 0, 0, -1, 1, 2, 0, -1, 1, 2)[n]
        column = (a + shift + SIDE) % SIDE
        if n == 1:
            ref = buf.at[s * SIDE + (a + back + SIDE) % SIDE, rows]
        elif n < 6:
            ref = buf.at[s * SIDE + column]
        else:
            ref = buf.at[(s + back + SIDE) % SIDE * SIDE + column, rows]
        device = ((right1, left1), (right2, left2))[n >= 2][side]
        at = (f * 10 + n) * 2 + side
        return remote(ref, ref, line_send.at[at], line_recv.at[at], device)

    def spread(f, *steps):
        for n in steps:
            for side in range(2):
                line_copy(f, n, side).start()

    def arrived(f, *steps):
        for n in steps:
            for side in range(2):
                line_copy(f, n, side).wait_recv()

    def load_kv(i):
        return pltpu.make_async_copy(
            kv_hbm.at[:, pl.ds(i * LANES, LANES)], kv_v.at[i], kv_sem.at[i]
        )

    load_near = pltpu.make_async_copy(near_hbm, near_v, load_sem.at[0])
    load_query = pltpu.make_async_copy(query_hbm, query_v, load_sem.at[1])
    load_uk = pltpu.make_async_copy(uk_hbm, uk_v, load_sem.at[2])
    load_uv = pltpu.make_async_copy(uv_hbm, uv_v, load_sem.at[3])
    for i in range(kv_v.shape[0]):
        load_kv(i).start()
    load_near.start()
    load_query.start()
    load_uk.start()
    load_uv.start()

    barrier = pltpu.get_barrier_semaphore()
    partners = (
        up, down, along_z(3), along_z(-3), to_twin, right1, left1, right2, left2, to_right, to_left,
    )
    for partner in partners:
        pl.semaphore_signal(barrier, inc=1, device_id=partner, device_id_type=MESH)

    low = lax.broadcasted_iota(jnp.int32, (WIDTH, LANES), 1) < BLOCK

    def selected_below(row, bound):
        found = jnp.int32(0)
        for i in range(selected):
            found += jnp.where(sel_ref[row, i] < bound, 1, 0)
        return found

    def pack(source, holder, starts, pair, out):
        def fetch(flip, slot):
            row = 2 * pair + flip
            at = jnp.minimum(starts(flip) + slot, selected - 1)
            block = jnp.clip(sel_ref[row, at] - holder * kb_dev, 0, kb_dev - 1)
            return source[block >> 1], block & 1

        for slot in range(CAP):
            tile, odd = fetch(core, slot)
            left = jnp.where(odd == 1, swap_halves(tile), tile)
            tile, odd = fetch(1 - core, slot)
            right = jnp.where(odd == 0, swap_halves(tile), tile)
            slots_v[out, slot] = jnp.where(low, left, right)

    first_own = [selected_below(row, kv * kb_dev) for row in range(blocks)]
    pl.semaphore_wait(barrier, len(partners))
    chain_copy(0).start()
    for i in range(kv_v.shape[0]):
        load_kv(i).wait()
    for pair in range(pairs):
        pack(
            kv_v, kv,
            lambda flip: jnp.where(flip == 0, first_own[2 * pair], first_own[2 * pair + 1]),
            pair, pair,
        )
        twin_copy(pair).start()
        if pair == 0:
            z_go(0)

    load_near.wait()
    near_copy = remote(near_v.at[:, pl.ds(tok - LANES, LANES)], before_v, near_send, near_recv, to_right)
    near_copy.start()

    load_query.wait()
    load_uk.wait()
    share = kv_total // (heads // 2)

    def prepare(j, _):
        full = []
        for i in range(2):
            h = 2 * j + i
            absorbed = transposed_dot(uk_v[h], query_v[h, :NOPE, :]).astype(BF16)
            full.append(jnp.concatenate([absorbed, query_v[h, NOPE:, :]], axis=0))
        column = pl.ds(pl.multiple_of(j * LANES, LANES), LANES)
        for pair in range(pairs):
            p = full[0][:, pair * LANES : (pair + 1) * LANES]
            q = full[1][:, pair * LANES : (pair + 1) * LANES]
            full_v[2 * pair, :, column] = jnp.where(low, p, swap_halves(q))
            full_v[2 * pair + 1, :, column] = jnp.where(low, swap_halves(p), q)
        for row in range(blocks):
            below = selected_below(row, j * share * kb_dev)
            for i in range(share):
                holder = j * share + i
                upto = selected_below(row, (holder + 1) * kb_dev)
                start_ref[row, holder] = below
                count_ref[row, holder] = upto - below
                below = upto

        return 0

    lax.fori_loop(0, heads // 2, prepare, 0)

    chain_copy(0).wait_recv()
    chain_copy(1).start()
    spread(0, 0, 2)
    z_go(1)

    rows = heads * BLOCK
    near_copy.wait_recv()
    token = lax.broadcasted_iota(jnp.int32, (BLOCK, rows), 1) % BLOCK
    entry = lax.broadcasted_iota(jnp.int32, (BLOCK, rows), 0)
    causal = entry <= token
    for row in range(blocks):
        tile = near_v[:, (row // 2) * LANES : (row // 2 + 1) * LANES]
        if row % 2 == 0:
            other = before_v[...] if row == 0 else near_v[:, (row // 2 - 1) * LANES : (row // 2) * LANES]
            tile = jnp.where(low, tile, other)
        scores = transposed_dot(tile, full_v[row]) * scale
        first, second = scores[:BLOCK], scores[BLOCK:]
        if row % 2 == 0:
            first = jnp.where(causal, first, NEG)
            if row == 0:
                second = jnp.where(pb > 0, second, NEG)
        else:
            second = jnp.where(causal, second, NEG)
        scores = jnp.concatenate([first, second], axis=0)
        top = jnp.max(scores, axis=0, keepdims=True)
        weights = jnp.exp2(scores - top)
        top_v[row] = top
        total_v[row] = jnp.sum(weights, axis=0, keepdims=True)
        acc_v[row] = jnp.dot(tile[:LATENT], weights.astype(BF16), preferred_element_type=F32)

    def place_of(slot):
        group, odd = slot // 2, slot % 2
        near = group % 2 == 1
        pair = jnp.where(near, group // 2 % 2, odd)
        reach = jnp.where(group >= 4, 2, 1)
        steps = jnp.where(near, (2 * odd - 1) * reach, 0)
        far_steps = jnp.where(near | (group == 0), 0, -2 - group // 2)
        return pair, steps, far_steps

    def holder_at(steps, far_steps, which):
        return 2 * ((chip + steps + far_steps * (1 - 2 * which) + 2 * chips) % chips) + which

    def fold(slot):
        pair, steps, far_steps = place_of(slot)
        mine = holder_at(steps, far_steps, core)
        other = holder_at(steps, far_steps, 1 - core)
        mine_low = [core == half for half in range(2)]
        all_keys, all_scores, all_weights = [], [], []
        for half in range(2):
            tiles = [jnp.where(low == mine_low[half], slots_v[slot, c], twin_v[slot, c]) for c in range(CAP)]
            keys = jnp.concatenate(tiles, axis=1)
            all_keys.append(keys)
            all_scores.append(transposed_dot(keys, full_v[2 * pair + half]))
        for half in range(2):
            row = 2 * pair + half
            low_count = jnp.where(mine_low[half], count_ref[row, mine], count_ref[row, other])
            high_count = jnp.where(mine_low[half], count_ref[row, other], count_ref[row, mine])
            scores = all_scores[half]
            parts = []
            for c in range(CAP):
                at = 2 * c * BLOCK
                low_bias = jnp.where(low_count > c, 0.0, NEG)
                high_bias = jnp.where(high_count > c, 0.0, NEG)
                parts.append(scores[at : at + BLOCK] * scale + low_bias)
                parts.append(scores[at + BLOCK : at + 2 * BLOCK] * scale + high_bias)
            scores = jnp.concatenate(parts, axis=0)
            old = top_v[row]
            top = jnp.maximum(old, jnp.max(scores, axis=0, keepdims=True))
            weights = jnp.exp2(scores - top)
            factor = jnp.exp2(old - top)
            top_v[row] = top
            total_v[row] = total_v[row] * factor + jnp.sum(weights, axis=0, keepdims=True)
            all_weights.append((weights.astype(BF16), factor))
        for half in range(2):
            row = 2 * pair + half
            weights, factor = all_weights[half]
            acc_v[row] = acc_v[row] * factor + jnp.dot(
                all_keys[half][:LATENT], weights, preferred_element_type=F32
            )

    def z_arrived(first, slot):
        for n in range(first, first + CAP):
            for side in range(2):
                z_copy(n, side).wait_recv()
            if n < 2 * CAP:
                z_go(n + 2 * CAP)
        for side in range(2):
            twin_copy(slot + side).start()

    def far_arrived(f):
        arrived(f, 6, 7, 8, 9)
        holder = holder_at(0, -(3 + f), core)
        for pair in range(pairs):
            out = 4 + 4 * f + pair
            pack(far_v[f], holder, lambda flip: start_ref[2 * pair + flip, holder], pair, out)
            twin_copy(out).start()

    def chained(f):
        chain_copy(f).wait_recv()
        if f < 2:
            chain_copy(f + 1).start()
        spread(f, 0, 2)

    def beside(f):
        arrived(f, 0)
        spread(f, 1, 3, 4)

    def opposite(f):
        arrived(f, 1)
        spread(f, 5)

    def cross(f, *steps):
        arrived(f, *steps)
        spread(f, *[n + 4 for n in steps])

    def then(*call):
        return functools.partial(*call)

    events = {
        0: [then(beside, 0), then(chained, 1), then(z_go, 2, 3, 4, 5)],
        1: [then(opposite, 0), then(chained, 2), then(beside, 1), then(cross, 0, 2, 3, 4)],
        2: [then(opposite, 1), then(cross, 0, 5), then(z_arrived, 0, 2), then(beside, 2)],
        3: [then(cross, 1, 2, 3, 4), then(opposite, 2)],
        4: [then(far_arrived, 0), then(cross, 1, 5)],
        5: [then(z_arrived, 3, 6), then(cross, 2, 2, 3, 4)],
        6: [then(cross, 2, 5)],
        7: [then(far_arrived, 1)],
        9: [then(z_arrived, 6, 10)],
        11: [then(far_arrived, 2)],
        13: [then(z_arrived, 9, 14)],
    }

    def stage(slot, _):
        for at, todo in events.items():
            @pl.when(slot == at)
            def _():
                for event in todo:
                    event()

        twin_copy(slot).wait_recv()
        fold(slot)
        return 0

    lax.fori_loop(0, chips * pairs, stage, 0)

    load_uv.wait()
    for row in range(blocks):
        latent = (acc_v[row] * (1.0 / total_v[row])).astype(BF16)
        for j in range(heads // 2):
            tile = latent[:, j * LANES : (j + 1) * LANES].T
            for i in range(2):
                latent_v[2 * j + i, row * BLOCK : (row + 1) * BLOCK, :] = tile[i * BLOCK : (i + 1) * BLOCK]
    for h in range(heads):
        out_ref[:, h * VDIM : (h + 1) * VDIM] = jnp.dot(
            latent_v[h], uv_v[h], preferred_element_type=F32
        ).astype(BF16)

    near_copy.wait_send()
    for n in range(4 * CAP):
        for side in range(2):
            z_copy(n, side).wait_send()
    for slot in range(chips * pairs):
        twin_copy(slot).wait_send()
    for f in range(len(far_v)):
        chain_copy(f).wait_send()
        for n in range(10):
            for side in range(2):
                line_copy(f, n, side).wait_send()


def per_device(query, w_uk, w_uv, kv_cache, stretch_latent, selection):
    pb_total = lax.axis_size("pb")
    kv_total = lax.axis_size("kv")
    tok, heads, qwidth = query.shape
    blocks = tok // BLOCK
    pairs = blocks // 2
    chips = kv_total // 2
    scale = math.log2(math.e) / math.sqrt(qwidth)
    slots = chips * pairs
    smem = pl.BlockSpec(memory_space=pltpu.SMEM)
    anywhere = pl.BlockSpec(memory_space=pl.ANY)
    dma = pltpu.SemaphoreType.DMA
    return pl.pallas_call(
        functools.partial(kernel, pb_total, kv_total, scale),
        out_shape=jax.ShapeDtypeStruct((tok, heads * VDIM), BF16),
        in_specs=[smem] + [anywhere] * 5,
        out_specs=pl.BlockSpec(memory_space=pltpu.VMEM),
        scratch_shapes=[
            *[pltpu.VMEM((kv_cache.shape[0] // LANES, WIDTH, LANES), BF16)] * 4,
            pltpu.VMEM((heads, qwidth, tok), BF16),
            pltpu.VMEM(w_uk.shape, BF16),
            pltpu.VMEM(w_uv.shape, BF16),
            pltpu.VMEM((WIDTH, tok), BF16),
            pltpu.VMEM((WIDTH, LANES), BF16),
            pltpu.VMEM((blocks, WIDTH, heads * BLOCK), BF16),
            pltpu.VMEM((slots, CAP, WIDTH, LANES), BF16),
            pltpu.VMEM((slots, CAP, WIDTH, LANES), BF16),
            pltpu.VMEM((blocks, LATENT, heads * BLOCK), F32),
            pltpu.VMEM((blocks, 1, heads * BLOCK), F32),
            pltpu.VMEM((blocks, 1, heads * BLOCK), F32),
            pltpu.VMEM((heads, tok, LATENT), BF16),
            pltpu.SMEM((blocks, kv_total), jnp.int32),
            pltpu.SMEM((blocks, kv_total), jnp.int32),
            dma((4,)),
            dma((kv_cache.shape[0] // LANES,)),
            dma,
            dma,
            dma((8 * CAP,)),
            dma((8 * CAP,)),
            dma((slots,)),
            dma((slots,)),
            dma((3,)),
            dma((3,)),
            dma((60,)),
            dma((60,)),
        ],
        compiler_params=pltpu.CompilerParams(
            collective_id=0, has_side_effects=True, vmem_limit_bytes=56 * 1024 * 1024
        ),
        cost_estimate=pl.CostEstimate(
            flops=2 * blocks * heads * BLOCK * 3200 * (WIDTH + LATENT),
            bytes_accessed=8 * 1024 * 1024,
            transcendentals=blocks * heads * BLOCK * 3200,
        ),
    )(
        selection,
        jnp.transpose(query, (1, 2, 0)),
        w_uk,
        w_uv,
        kv_cache.T,
        stretch_latent.T,
    )


def solution(mesh):
    placed = (
        P("pb", "kv", None),
        P("kv", None, None),
        P("kv", None, None),
        P("kv", None),
        P("pb", None),
        P("pb", None),
    )
    return jax.shard_map(
        per_device, mesh=mesh, in_specs=placed, out_specs=P("pb", "kv"), check_vma=False
    )
```

```python
import functools
import math

import jax
import jax.numpy as jnp
from jax import lax
from jax.experimental import pallas as pl
from jax.experimental.pallas import tpu as pltpu
from jax.sharding import PartitionSpec as P

NOPE = 128
ROPE = 64
LATENT = 512
WIDTH = LATENT + ROPE
VDIM = 128
BLOCK = 64
LANES = 128
CAP = 3
SIDE = 4
NEG = -1e30
MESH = pl.DeviceIdType.MESH
F32 = jnp.float32
BF16 = jnp.bfloat16


def transposed_dot(a, b):
    return lax.dot_general(a, b, (((0,), (0,)), ((), ())), preferred_element_type=F32)


def swap_halves(x):
    return jnp.concatenate([x[:, BLOCK:], x[:, :BLOCK]], axis=1)


def kernel(
    pb_total, kv_total, scale,
    sel_ref, query_hbm, uk_hbm, uv_hbm, kv_hbm, near_hbm,
    out_ref,
    kv_v, far0_v, far1_v, far2_v, query_v, uk_v, uv_v, near_v, before_v, full_v, slots_v, twin_v,
    acc_v, top_v, total_v, latent_v, start_ref, count_ref,
    load_sem, kv_sem, near_send, near_recv, z_send, z_recv, twin_send, twin_recv,
    chain_send, chain_recv, line_send, line_recv,
):
    far_v = (far0_v, far1_v, far2_v)
    heads = query_v.shape[0]
    tok = query_v.shape[2]
    blocks = tok // BLOCK
    pairs = blocks // 2
    chips = kv_total // 2
    kb_dev = 2 * kv_v.shape[0]
    selected = sel_ref.shape[1]
    pb = lax.axis_index("pb")
    kv = lax.axis_index("kv")
    chip = kv // 2
    core = kv % 2
    turn = 1 - 2 * core
    half_width = WIDTH // 2

    def along_z(steps):
        return (pb, 2 * ((chip + steps + 2 * chips) % chips) + core)

    x, y = pb % SIDE, pb // SIDE
    a = (1 - core) * x + core * y
    s = (1 - core) * y + core * x
    place = s * SIDE + a

    def plane(da, ds):
        na, ns = (a + da + SIDE) % SIDE, (s + ds + SIDE) % SIDE
        return ((1 - core) * (ns * SIDE + na) + core * (na * SIDE + ns), kv)

    to_twin = (pb, 2 * chip + 1 - core)
    up, down = along_z(1), along_z(-1)
    right1, left1, right2, left2 = plane(1, 0), plane(-1, 0), plane(0, 1), plane(0, -1)
    to_right = ((pb + 1) % pb_total, kv)
    to_left = ((pb + pb_total - 1) % pb_total, kv)

    def remote(src, dst, send_sem, recv_sem, device):
        return pltpu.make_async_remote_copy(
            src_ref=src, dst_ref=dst, send_sem=send_sem, recv_sem=recv_sem,
            device_id=device, device_id_type=MESH,
        )

    def z_copy(n, side):
        pair, c = n // CAP % 2, n % CAP
        first = 2 + 4 * pair + side
        src, dst = (pair, first) if n < 2 * CAP else (first, 10 + 4 * pair + side)
        at = 2 * n + side
        return remote(
            slots_v.at[src, c], slots_v.at[dst, c], z_send.at[at], z_recv.at[at], (up, down)[side]
        )

    def z_go(*tiles):
        for n in tiles:
            for side in range(2):
                z_copy(n, side).start()

    def twin_copy(slot):
        return remote(slots_v.at[slot], twin_v.at[slot], twin_send.at[slot], twin_recv.at[slot], to_twin)

    def chain_copy(f):
        tile = kv_hbm.at[:, pl.ds(place * LANES, LANES)] if f == 0 else far_v[f - 1].at[place]
        return remote(
            tile, far_v[f].at[place], chain_send.at[f], chain_recv.at[f],
            along_z(3 * turn if f == 0 else turn),
        )

    def line_copy(f, n, side):
        buf = far_v[f]
        back = 2 * side - 1
        rows = pl.ds(side * half_width, half_width)
        shift = (0, 0, 0, -1, 1, 2, 0, -1, 1, 2)[n]
        column = (a + shift + SIDE) % SIDE
        if n == 1:
            ref = buf.at[s * SIDE + (a + back + SIDE) % SIDE, rows]
        elif n < 6:
            ref = buf.at[s * SIDE + column]
        else:
            ref = buf.at[(s + back + SIDE) % SIDE * SIDE + column, rows]
        device = ((right1, left1), (right2, left2))[n >= 2][side]
        at = (f * 10 + n) * 2 + side
        return remote(ref, ref, line_send.at[at], line_recv.at[at], device)

    def spread(f, *steps):
        for n in steps:
            for side in range(2):
                line_copy(f, n, side).start()

    def arrived(f, *steps):
        for n in steps:
            for side in range(2):
                line_copy(f, n, side).wait_recv()

    def load_kv(i):
        return pltpu.make_async_copy(
            kv_hbm.at[:, pl.ds(i * LANES, LANES)], kv_v.at[i], kv_sem.at[i]
        )

    barrier = pltpu.get_barrier_semaphore()
    partners = (
        up, down, along_z(3), along_z(-3), to_twin, right1, left1, right2, left2, to_right, to_left,
    )
    for partner in partners:
        pl.semaphore_signal(barrier, inc=1, device_id=partner, device_id_type=MESH)

    load_near = pltpu.make_async_copy(near_hbm, near_v, load_sem.at[0])
    load_query = pltpu.make_async_copy(query_hbm, query_v, load_sem.at[1])
    load_uk = pltpu.make_async_copy(uk_hbm, uk_v, load_sem.at[2])
    load_uv = pltpu.make_async_copy(uv_hbm, uv_v, load_sem.at[3])
    for i in range(kv_v.shape[0]):
        load_kv(i).start()
    load_near.start()
    load_query.start()
    load_uk.start()
    load_uv.start()

    low = lax.broadcasted_iota(jnp.int32, (WIDTH, LANES), 1) < BLOCK

    def selected_below(row, bound):
        found = jnp.int32(0)
        for i in range(selected):
            found += jnp.where(sel_ref[row, i] < bound, 1, 0)
        return found

    def pack(source, holder, starts, pair, out):
        def fetch(flip, slot):
            row = 2 * pair + flip
            at = jnp.minimum(starts(flip) + slot, selected - 1)
            block = jnp.clip(sel_ref[row, at] - holder * kb_dev, 0, kb_dev - 1)
            return source[block >> 1], block & 1

        for slot in range(CAP):
            tile, odd = fetch(core, slot)
            left = jnp.where(odd == 1, swap_halves(tile), tile)
            tile, odd = fetch(1 - core, slot)
            right = jnp.where(odd == 0, swap_halves(tile), tile)
            slots_v[out, slot] = jnp.where(low, left, right)

    pl.semaphore_wait(barrier, len(partners))
    chain_copy(0).start()
    first_own = [selected_below(row, kv * kb_dev) for row in range(blocks)]
    for i in range(kv_v.shape[0]):
        load_kv(i).wait()
    for pair in range(pairs):
        pack(
            kv_v, kv,
            lambda flip: jnp.where(flip == 0, first_own[2 * pair], first_own[2 * pair + 1]),
            pair, pair,
        )
        twin_copy(pair).start()
        if pair == 0:
            z_go(0)

    load_near.wait()
    near_copy = remote(near_v.at[:, pl.ds(tok - LANES, LANES)], before_v, near_send, near_recv, to_right)
    near_copy.start()

    load_query.wait()
    load_uk.wait()
    share = kv_total // (heads // 2)

    def prepare(j, _):
        full = []
        for i in range(2):
            h = 2 * j + i
            absorbed = transposed_dot(uk_v[h], query_v[h, :NOPE, :]).astype(BF16)
            full.append(jnp.concatenate([absorbed, query_v[h, NOPE:, :]], axis=0))
        column = pl.ds(pl.multiple_of(j * LANES, LANES), LANES)
        for pair in range(pairs):
            p = full[0][:, pair * LANES : (pair + 1) * LANES]
            q = full[1][:, pair * LANES : (pair + 1) * LANES]
            full_v[2 * pair, :, column] = jnp.where(low, p, swap_halves(q))
            full_v[2 * pair + 1, :, column] = jnp.where(low, swap_halves(p), q)
        for row in range(blocks):
            below = selected_below(row, j * share * kb_dev)
            for i in range(share):
                holder = j * share + i
                upto = selected_below(row, (holder + 1) * kb_dev)
                start_ref[row, holder] = below
                count_ref[row, holder] = upto - below
                below = upto

        return 0

    lax.fori_loop(0, heads // 2, prepare, 0)

    chain_copy(0).wait_recv()
    chain_copy(1).start()
    spread(0, 0, 2)
    z_go(1)

    rows = heads * BLOCK
    near_copy.wait_recv()
    token = lax.broadcasted_iota(jnp.int32, (BLOCK, rows), 1) % BLOCK
    entry = lax.broadcasted_iota(jnp.int32, (BLOCK, rows), 0)
    causal = entry <= token
    for row in range(blocks):
        tile = near_v[:, (row // 2) * LANES : (row // 2 + 1) * LANES]
        if row % 2 == 0:
            other = before_v[...] if row == 0 else near_v[:, (row // 2 - 1) * LANES : (row // 2) * LANES]
            tile = jnp.where(low, tile, other)
        scores = transposed_dot(tile, full_v[row]) * scale
        first, second = scores[:BLOCK], scores[BLOCK:]
        if row % 2 == 0:
            first = jnp.where(causal, first, NEG)
            if row == 0:
                second = jnp.where(pb > 0, second, NEG)
        else:
            second = jnp.where(causal, second, NEG)
        scores = jnp.concatenate([first, second], axis=0)
        top = jnp.max(scores, axis=0, keepdims=True)
        weights = jnp.exp2(scores - top)
        top_v[row] = top
        total_v[row] = jnp.sum(weights, axis=0, keepdims=True)
        acc_v[row] = jnp.dot(tile[:LATENT], weights.astype(BF16), preferred_element_type=F32)

    def place_of(slot):
        group, odd = slot // 2, slot % 2
        near = group % 2 == 1
        pair = jnp.where(near, group // 2 % 2, odd)
        reach = jnp.where(group >= 4, 2, 1)
        steps = jnp.where(near, (2 * odd - 1) * reach, 0)
        far_steps = jnp.where(near | (group == 0), 0, -2 - group // 2)
        return pair, steps, far_steps

    def holder_at(steps, far_steps, which):
        return 2 * ((chip + steps + far_steps * (1 - 2 * which) + 2 * chips) % chips) + which

    def fold(slot):
        pair, steps, far_steps = place_of(slot)
        mine = holder_at(steps, far_steps, core)
        other = holder_at(steps, far_steps, 1 - core)
        mine_low = [core == half for half in range(2)]
        all_keys, all_scores, all_weights = [], [], []
        for half in range(2):
            tiles = [jnp.where(low == mine_low[half], slots_v[slot, c], twin_v[slot, c]) for c in range(CAP)]
            keys = jnp.concatenate(tiles, axis=1)
            all_keys.append(keys)
            all_scores.append(transposed_dot(keys, full_v[2 * pair + half]))
        for half in range(2):
            row = 2 * pair + half
            low_count = jnp.where(mine_low[half], count_ref[row, mine], count_ref[row, other])
            high_count = jnp.where(mine_low[half], count_ref[row, other], count_ref[row, mine])
            scores = all_scores[half]
            biases = []
            for c in range(CAP):
                biases.append(jnp.where(low_count > c, 0.0, NEG))
                biases.append(jnp.where(high_count > c, 0.0, NEG))
            scores = scores * scale
            parts = [scores[n * BLOCK : (n + 1) * BLOCK] for n in range(2 * CAP)]
            old = top_v[row]
            top = old
            for part, bias in zip(parts, biases):
                top = jnp.maximum(top, jnp.max(part, axis=0, keepdims=True) + bias)
            weights = jnp.concatenate(
                [jnp.exp2(part - (top - bias)) for part, bias in zip(parts, biases)], axis=0
            )
            factor = jnp.exp2(old - top)
            top_v[row] = top
            total_v[row] = total_v[row] * factor + jnp.sum(weights, axis=0, keepdims=True)
            all_weights.append((weights.astype(BF16), factor))
        for half in range(2):
            row = 2 * pair + half
            weights, factor = all_weights[half]
            acc_v[row] = acc_v[row] * factor + jnp.dot(
                all_keys[half][:LATENT], weights, preferred_element_type=F32
            )

    def z_arrived(first, slot):
        for n in range(first, first + CAP):
            for side in range(2):
                z_copy(n, side).wait_recv()
            if n < 2 * CAP:
                z_go(n + 2 * CAP)
        for side in range(2):
            twin_copy(slot + side).start()

    def far_arrived(f):
        arrived(f, 6, 7, 8, 9)
        holder = holder_at(0, -(3 + f), core)
        for pair in range(pairs):
            out = 4 + 4 * f + pair
            pack(far_v[f], holder, lambda flip: start_ref[2 * pair + flip, holder], pair, out)
            twin_copy(out).start()

    def chained(f):
        chain_copy(f).wait_recv()
        if f < 2:
            chain_copy(f + 1).start()
        spread(f, 0, 2)

    def beside(f):
        arrived(f, 0)
        spread(f, 1, 3, 4)

    def opposite(f):
        arrived(f, 1)
        spread(f, 5)

    def cross(f, *steps):
        arrived(f, *steps)
        spread(f, *[n + 4 for n in steps])

    def then(*call):
        return functools.partial(*call)

    events = {
        0: [then(beside, 0), then(chained, 1), then(z_go, 2, 3, 4, 5)],
        1: [then(opposite, 0), then(chained, 2), then(beside, 1), then(cross, 0, 2, 3, 4)],
        2: [then(opposite, 1), then(cross, 0, 5), then(z_arrived, 0, 2), then(beside, 2)],
        3: [then(cross, 1, 2, 3, 4), then(opposite, 2)],
        4: [then(far_arrived, 0), then(cross, 1, 5)],
        5: [then(z_arrived, 3, 6), then(cross, 2, 2, 3, 4)],
        6: [then(cross, 2, 5)],
        7: [then(far_arrived, 1)],
        9: [then(z_arrived, 6, 10)],
        11: [then(far_arrived, 2)],
        13: [then(z_arrived, 9, 14)],
    }

    def stage(slot, _):
        for at, todo in events.items():
            @pl.when(slot == at)
            def _():
                for event in todo:
                    event()

        twin_copy(slot).wait_recv()
        fold(slot)
        return 0

    lax.fori_loop(0, chips * pairs, stage, 0)

    load_uv.wait()
    for row in range(blocks):
        latent = (acc_v[row] * (1.0 / total_v[row])).astype(BF16)
        for j in range(heads // 2):
            tile = latent[:, j * LANES : (j + 1) * LANES].T
            for i in range(2):
                latent_v[2 * j + i, row * BLOCK : (row + 1) * BLOCK, :] = tile[i * BLOCK : (i + 1) * BLOCK]
    for h in range(heads):
        out_ref[:, h * VDIM : (h + 1) * VDIM] = jnp.dot(
            latent_v[h], uv_v[h], preferred_element_type=F32
        ).astype(BF16)

    near_copy.wait_send()
    for n in range(4 * CAP):
        for side in range(2):
            z_copy(n, side).wait_send()
    for slot in range(chips * pairs):
        twin_copy(slot).wait_send()
    for f in range(len(far_v)):
        chain_copy(f).wait_send()
        for n in range(10):
            for side in range(2):
                line_copy(f, n, side).wait_send()


def per_device(query, w_uk, w_uv, kv_cache, stretch_latent, selection):
    pb_total = lax.axis_size("pb")
    kv_total = lax.axis_size("kv")
    tok, heads, qwidth = query.shape
    blocks = tok // BLOCK
    pairs = blocks // 2
    chips = kv_total // 2
    scale = math.log2(math.e) / math.sqrt(qwidth)
    slots = chips * pairs
    smem = pl.BlockSpec(memory_space=pltpu.SMEM)
    anywhere = pl.BlockSpec(memory_space=pl.ANY)
    dma = pltpu.SemaphoreType.DMA
    return pl.pallas_call(
        functools.partial(kernel, pb_total, kv_total, scale),
        out_shape=jax.ShapeDtypeStruct((tok, heads * VDIM), BF16),
        in_specs=[smem] + [anywhere] * 5,
        out_specs=pl.BlockSpec(memory_space=pltpu.VMEM),
        scratch_shapes=[
            *[pltpu.VMEM((kv_cache.shape[0] // LANES, WIDTH, LANES), BF16)] * 4,
            pltpu.VMEM((heads, qwidth, tok), BF16),
            pltpu.VMEM(w_uk.shape, BF16),
            pltpu.VMEM(w_uv.shape, BF16),
            pltpu.VMEM((WIDTH, tok), BF16),
            pltpu.VMEM((WIDTH, LANES), BF16),
            pltpu.VMEM((blocks, WIDTH, heads * BLOCK), BF16),
            pltpu.VMEM((slots, CAP, WIDTH, LANES), BF16),
            pltpu.VMEM((slots, CAP, WIDTH, LANES), BF16),
            pltpu.VMEM((blocks, LATENT, heads * BLOCK), F32),
            pltpu.VMEM((blocks, 1, heads * BLOCK), F32),
            pltpu.VMEM((blocks, 1, heads * BLOCK), F32),
            pltpu.VMEM((heads, tok, LATENT), BF16),
            pltpu.SMEM((blocks, kv_total), jnp.int32),
            pltpu.SMEM((blocks, kv_total), jnp.int32),
            dma((4,)),
            dma((kv_cache.shape[0] // LANES,)),
            dma,
            dma,
            dma((8 * CAP,)),
            dma((8 * CAP,)),
            dma((slots,)),
            dma((slots,)),
            dma((3,)),
            dma((3,)),
            dma((60,)),
            dma((60,)),
        ],
        compiler_params=pltpu.CompilerParams(
            collective_id=0, has_side_effects=True, vmem_limit_bytes=56 * 1024 * 1024
        ),
        cost_estimate=pl.CostEstimate(
            flops=2 * blocks * heads * BLOCK * 3200 * (WIDTH + LATENT),
            bytes_accessed=8 * 1024 * 1024,
            transcendentals=blocks * heads * BLOCK * 3200,
        ),
    )(
        selection,
        jnp.transpose(query, (1, 2, 0)),
        w_uk,
        w_uv,
        kv_cache.T,
        stretch_latent.T,
    )


def solution(mesh):
    placed = (
        P("pb", "kv", None),
        P("kv", None, None),
        P("kv", None, None),
        P("kv", None),
        P("pb", None),
        P("pb", None),
    )
    return jax.shard_map(
        per_device, mesh=mesh, in_specs=placed, out_specs=P("pb", "kv"), check_vma=False
    )
```
